1024 devices in a mesh: graph: 128 (over z, x), feat: 8 (over y, core).
Axes of the slice: x: 4, y: 4, z: 32, core: 2. Of those that a mesh axis runs over, the one named last changes fastest.
Arguments:
- features: bfloat16 [128, 1048576], P('feat', 'graph'), may hold values from -6 to 6
- w_self: bfloat16 [128, 128], replicated, may hold values from -0.5 to 0.5
- w_neigh: bfloat16 [128, 128], replicated, may hold values from -0.5 to 0.5
- bias: float32 [128], replicated, may hold values from -3 to 3
- hub_pick: int32 [256], P('graph'), may hold values from 0 to 63
- halo_send: int32 [2048], P('graph'), may hold values from 0 to 63
- tile_dst: int32 [32768], P('graph'), may hold values from 0 to 63
- tile_src: int32 [32768], P('graph'), may hold values from 0 to 335, as said below
- tile_edges: int32 [32768], P('graph'), may hold values from 1 to 128, as said below
- tile_count: int32 [128], P('graph'), may hold values from 64 to 256, as said below
- edge_src: int32 [32768, 128], P('graph'), may hold values from 0 to 127
- edge_dst: int32 [32768, 128], P('graph'), may hold values from 0 to 127
Outputs:
- updated: bfloat16 [128, 1048576], P('feat', 'graph')
The draws below stay inside these ranges and needn't reach their ends.
Inputs may be any that keep to these rules, and one draw needn't show every extreme that they name: `tile_src`: A tile's source index counts into table_p: below 64 own blocks, then 256 hub blocks, then 2 * 8 halo blocks; the largest value occurs in every draw. `tile_edges`: some tile of every draw has all 128 slots live. `tile_count`: some partition of every draw has all 256 tiles live.
All inputs are finite; a program needn't handle non-finite values.
Results may differ from the reference program's by a relative error of at most 0.0015.
Values may be sent and summed in bfloat16 or wider, within the bound.
No kernel may reach another device: no remote copies, remote signals or barrier semaphores. Data moves between devices by JAX's collectives and lax.ppermute only.
A program may use at most 64 MiB of HBM per device.

```python
import jax
import jax.numpy as jnp
from jax import lax

F = 128
BLOCK = 128
EDGES = 128
NB_DEV = 64
HUB_DEV = 2
HALO = 8
TILES_DEV = 256
HUBS = 256
SLOTS = 336
NODES = 1048576
N_GRAPH = 128


def draw_tile_src(key, part):
    key = jax.random.fold_in(key, 11)
    kinds, local_key, hub_key, halo_key, spot_key = jax.random.split(key, 5)
    total = N_GRAPH * TILES_DEV
    category = jax.random.randint(kinds, (total,), 0, 4)
    local_slot = jax.random.randint(local_key, (total,), 0, NB_DEV)
    hub_slot = NB_DEV + jax.random.randint(hub_key, (total,), 0, HUBS)
    halo_slot = NB_DEV + HUBS + jax.random.randint(halo_key, (total,), 0, 2 * HALO)
    slots = jnp.where(category < 2, local_slot, jnp.where(category == 2, hub_slot, halo_slot))
    spot = jax.random.randint(spot_key, (), 0, total)
    return slots.at[spot].set(SLOTS - 1).astype(jnp.int32)


def draw_tile_edges(key, part):
    key = jax.random.fold_in(key, 23)
    count_key, spot_key = jax.random.split(key)
    total = N_GRAPH * TILES_DEV
    counts = jax.random.randint(count_key, (total,), 1, EDGES + 1)
    spot = jax.random.randint(spot_key, (), 0, total)
    return counts.at[spot].set(EDGES).astype(jnp.int32)


def draw_tile_count(key, part):
    key = jax.random.fold_in(key, 37)
    count_key, spot_key = jax.random.split(key)
    counts = jax.random.randint(count_key, (N_GRAPH,), TILES_DEV // 4, TILES_DEV + 1)
    spot = jax.random.randint(spot_key, (), 0, N_GRAPH)
    return counts.at[spot].set(TILES_DEV).astype(jnp.int32)


def set_ends(drawn, own_key, low, high):
    longest = drawn.shape.index(max(drawn.shape))
    spots = []
    for shift in (0, 1):
        where = [jax.random.randint(jax.random.fold_in(own_key, axis), (), 0, length) for axis, length in enumerate(drawn.shape)]
        where[longest] = (where[longest] + shift) % drawn.shape[longest]
        spots.append(tuple(where))
    return drawn.at[spots[0]].set(low).at[spots[1]].set(high)


def level_of(rng, dims, shards, smallest, high):
    gain = 1.0
    for axis_at, parts in shards:
        heights = jax.random.uniform(jax.random.fold_in(jax.random.fold_in(rng, 6), axis_at), (parts,), jnp.float32, smallest / len(shards), high / len(shards))
        gain = gain * jnp.repeat(jnp.exp(heights), dims[axis_at] // parts).reshape((-1,) + (1,) * (len(dims) - 1 - axis_at))
    return gain


def noise(stream_key, extent, width, most, shards=(), kind=jnp.bfloat16):
    loudness = level_of(stream_key, extent, shards, -0.22, 0.18) if shards else 1.0
    array = jax.random.normal(stream_key, extent, jnp.float32) * width * loudness
    return jnp.minimum(jnp.maximum(array, -most), most).astype(kind)


def setup_inputs(seed: int = 0) -> dict:
    keys = jax.random.split(jax.random.key(seed), 13)
    features = noise(keys[0], (F, NODES), 1.0, 6.0, ((0, 8), (1, 128)))
    w_self = noise(keys[1], (F, F), F ** -0.5, 0.5)
    w_neigh = noise(keys[2], (F, F), F ** -0.5, 0.5)
    bias = noise(keys[3], (F,), 0.5, 3.0, (), jnp.float32)
    hub_pick = set_ends(jax.random.randint(keys[4], (HUBS,), 0, NB_DEV), jax.random.fold_in(keys[4], 1), 0, NB_DEV - 1).astype(jnp.int32)
    halo_send = set_ends(jax.random.randint(keys[5], (N_GRAPH * 2 * HALO,), 0, NB_DEV), jax.random.fold_in(keys[5], 1), 0, NB_DEV - 1).astype(jnp.int32)
    tile_dst = set_ends(jax.random.randint(keys[6], (N_GRAPH * TILES_DEV,), 0, NB_DEV), jax.random.fold_in(keys[6], 1), 0, NB_DEV - 1).astype(jnp.int32)
    tile_src = draw_tile_src(jax.random.fold_in(keys[12], 71), 0)
    tile_edges = draw_tile_edges(jax.random.fold_in(keys[12], 71), 0)
    tile_count = draw_tile_count(jax.random.fold_in(keys[12], 71), 0)
    edge_src = set_ends(jax.random.randint(keys[10], (N_GRAPH * TILES_DEV, EDGES), 0, BLOCK), jax.random.fold_in(keys[10], 1), 0, BLOCK - 1).astype(jnp.int32)
    edge_dst = set_ends(jax.random.randint(keys[11], (N_GRAPH * TILES_DEV, EDGES), 0, BLOCK), jax.random.fold_in(keys[11], 1), 0, BLOCK - 1).astype(jnp.int32)
    return dict(features=features, w_self=w_self, w_neigh=w_neigh, bias=bias, hub_pick=hub_pick, halo_send=halo_send, tile_dst=tile_dst, tile_src=tile_src, tile_edges=tile_edges, tile_count=tile_count, edge_src=edge_src, edge_dst=edge_dst)


def partition_mean(blocks, hub_rows, halo_send, tile_dst, tile_src, tile_edges, tile_count, edge_src, edge_dst, partition):
    previous = (partition - 1) % N_GRAPH
    following = (partition + 1) % N_GRAPH
    left_list = lax.dynamic_slice_in_dim(halo_send, (previous * 2 * HALO + HALO).astype(jnp.int32), HALO)
    right_list = lax.dynamic_slice_in_dim(halo_send, (following * 2 * HALO).astype(jnp.int32), HALO)
    own_blocks = blocks[:, partition]
    left_rows = blocks[:, previous][:, left_list]
    right_rows = blocks[:, following][:, right_list]
    table = jnp.concatenate([own_blocks, hub_rows, left_rows, right_rows], axis=1).reshape(F, SLOTS * BLOCK)
    first_tile = (partition * TILES_DEV).astype(jnp.int32)
    dst_part = lax.dynamic_slice_in_dim(tile_dst, first_tile, TILES_DEV)
    src_part = lax.dynamic_slice_in_dim(tile_src, first_tile, TILES_DEV)
    edges_part = lax.dynamic_slice_in_dim(tile_edges, first_tile, TILES_DEV)
    esrc_part = lax.dynamic_slice_in_dim(edge_src, first_tile, TILES_DEV, 0)
    edst_part = lax.dynamic_slice_in_dim(edge_dst, first_tile, TILES_DEV, 0)
    source = (src_part[:, None] * BLOCK + esrc_part).reshape(-1)
    target = (dst_part[:, None] * BLOCK + edst_part).reshape(-1)
    live = (jnp.arange(EDGES, dtype=jnp.int32)[None, :] < edges_part[:, None]) & (jnp.arange(TILES_DEV, dtype=jnp.int32)[:, None] < tile_count[partition])
    live = live.reshape(-1)
    values = jnp.where(live[None, :], table[:, source].astype(jnp.float32), jnp.float32(0.0))
    sums = jnp.zeros((F, NB_DEV * BLOCK), jnp.float32).at[:, target].add(values)
    degree = jnp.zeros((NB_DEV * BLOCK,), jnp.float32).at[target].add(live.astype(jnp.float32))
    return (sums / jnp.maximum(degree, 1.0)[None, :]).astype(jnp.bfloat16)


def reference(features, w_self, w_neigh, bias, hub_pick, halo_send, tile_dst, tile_src, tile_edges, tile_count, edge_src, edge_dst):
    blocks = features.reshape(F, N_GRAPH, NB_DEV, BLOCK)
    owners = (jnp.arange(HUBS, dtype=jnp.int32) // HUB_DEV).astype(jnp.int32)
    hub_rows = blocks[:, owners, hub_pick]

    def one_partition(partition):
        return partition_mean(blocks, hub_rows, halo_send, tile_dst, tile_src, tile_edges, tile_count, edge_src, edge_dst, partition)

    means = lax.map(one_partition, jnp.arange(N_GRAPH, dtype=jnp.int32))
    mean = jnp.transpose(means, (1, 0, 2)).reshape(F, NODES)
    total = jnp.dot(w_self, features, preferred_element_type=jnp.float32) + jnp.dot(w_neigh, mean, preferred_element_type=jnp.float32)
    return jax.nn.relu(total + bias[:, None]).astype(jnp.bfloat16)
```

```python
import jax
import jax.numpy as jnp
from jax import lax
from jax.experimental import pallas as pl
from jax.experimental.pallas import tpu as pltpu
from jax.sharding import PartitionSpec as P

BLOCK = 128
GROUP = 8
Z, X = 32, 4
STRIDE = 2


def pick_kernel(hub_pick, halo_send, features, hub_out, halo_out):
    def copy(out, picks):
        for i in range(out.shape[0]):
            start = pl.multiple_of(picks[i] * BLOCK, BLOCK)
            out[i] = features[:, pl.ds(start, BLOCK)]

    copy(hub_out, hub_pick)
    copy(halo_out, halo_send)


def pick_blocks(features, hub_pick, halo_send):
    rows = features.shape[0]
    smem = pl.BlockSpec(memory_space=pltpu.SMEM)
    vmem = pl.BlockSpec(memory_space=pltpu.VMEM)
    return pl.pallas_call(
        pick_kernel,
        out_shape=[
            jax.ShapeDtypeStruct((hub_pick.shape[0], rows, BLOCK), features.dtype),
            jax.ShapeDtypeStruct((halo_send.shape[0], rows, BLOCK), features.dtype),
        ],
        in_specs=[smem, smem, vmem],
        out_specs=[vmem, vmem],
        name="pick_blocks",
    )(hub_pick, halo_send, features)


def table_row(slot, own, hubs):
    hub = slot - own
    group = X * STRIDE
    owner = hub >> 1
    place = ((owner & (group - 1)) * (hubs // group)) + ((owner // group) << 1) + (hub & 1)
    return jnp.where((hub >= 0) & (hub < hubs), own + place, slot)


def mean_kernel(
    tile_dst,
    tile_src,
    tile_edges,
    tile_count,
    features,
    edge_src,
    edge_dst,
    hub_rows,
    halo_low,
    halo_high,
    mean_out,
    table,
    sums,
    sems,
):
    rows = features.shape[0]
    own = features.shape[1] // BLOCK
    hubs = hub_rows.shape[0]
    halo = halo_low.shape[0]
    copies = [
        pltpu.make_async_copy(hub_rows, table.at[pl.ds(own, hubs)], sems.at[0]),
        pltpu.make_async_copy(halo_low, table.at[pl.ds(own + hubs, halo)], sems.at[1]),
        pltpu.make_async_copy(halo_high, table.at[pl.ds(own + hubs + halo, halo)], sems.at[2]),
    ]
    for copy in copies:
        copy.start()
    for b in range(own):
        table[b] = features[:, b * BLOCK : (b + 1) * BLOCK]
        sums[b] = jnp.zeros(sums.shape[1:], jnp.float32)
    for copy in copies:
        copy.wait()

    count = tile_count[0]
    lane = lax.broadcasted_iota(jnp.int32, (8, BLOCK), 1)
    node = lax.broadcasted_iota(jnp.int32, (BLOCK, BLOCK), 0)
    ones = jnp.ones((sums.shape[1] - rows, BLOCK), jnp.float32)

    @pl.loop(0, (count + GROUP - 1) // GROUP)
    def _(step):
        first = pl.multiple_of(step * GROUP, GROUP)
        sources = edge_src[pl.ds(first, GROUP), :]
        targets = edge_dst[pl.ds(first, GROUP), :]
        parts = []
        for i in range(GROUP):
            tile = first + i
            live = jnp.where(tile < count, tile_edges[tile], 0)
            block = table[table_row(tile_src[tile], own, hubs)].astype(jnp.float32)
            index = jnp.broadcast_to(sources[i : i + 1], (8, BLOCK))
            values = [
                jnp.take_along_axis(block[r : r + 8], index, axis=1, mode="promise_in_bounds")
                for r in range(0, rows, 8)
            ]
            left = jnp.concatenate(values + [ones], axis=0).astype(jnp.bfloat16)
            target = jnp.where(lane < live, jnp.broadcast_to(targets[i : i + 1], (8, BLOCK)), -1)
            hits = node == jnp.broadcast_to(target[:1], (BLOCK, BLOCK))
            right = jnp.where(hits, 1.0, 0.0).astype(jnp.bfloat16)
            parts.append(
                lax.dot_general(
                    left, right, (((1,), (1,)), ((), ())), preferred_element_type=jnp.float32
                )
            )
        for i in range(GROUP):
            place = tile_dst[first + i]
            sums[place] = sums[place] + parts[i]

    per = own // mean_out.shape[0]
    for b in range(own):
        total = sums[b]
        degree = jnp.maximum(total[rows : rows + 8], 1.0)
        mean = jnp.concatenate([total[r : r + 8] / degree for r in range(0, rows, 8)], axis=0)
        at = (b % per) * BLOCK
        mean_out[b // per, :, at : at + BLOCK] = mean.astype(mean_out.dtype)


def neighbour_mean(
    features, hub_rows, halo_low, halo_high, tile_dst, tile_src, tile_edges, tile_count, edge_src, edge_dst, parts
):
    rows, nodes = features.shape
    own = nodes // BLOCK
    slots = own + hub_rows.shape[0] + 2 * halo_low.shape[0]
    smem = pl.BlockSpec(memory_space=pltpu.SMEM)
    vmem = pl.BlockSpec(memory_space=pltpu.VMEM)
    anywhere = pl.BlockSpec(memory_space=pl.ANY)
    return pl.pallas_call(
        mean_kernel,
        out_shape=jax.ShapeDtypeStruct((parts, rows, nodes // parts), features.dtype),
        in_specs=[smem] * 4 + [vmem] * 3 + [anywhere] * 3,
        out_specs=vmem,
        scratch_shapes=[
            pltpu.VMEM((slots, rows, BLOCK), features.dtype),
            pltpu.VMEM((own, 2 * rows, BLOCK), jnp.float32),
            pltpu.SemaphoreType.DMA((3,)),
        ],
        compiler_params=pltpu.CompilerParams(vmem_limit_bytes=32 * 1024 * 1024),
        name="neighbour_mean",
    )(tile_dst, tile_src, tile_edges, tile_count, features, edge_src, edge_dst, hub_rows, halo_low, halo_high)


def project_kernel(features, mean, w_self, w_neigh, bias, out):
    total = jnp.dot(w_self[...], features[...], preferred_element_type=jnp.float32) + jnp.dot(
        w_neigh[...], mean[...], preferred_element_type=jnp.float32
    )
    out[...] = jnp.maximum(total + bias[...], 0.0).astype(out.dtype)


def project(features, mean, w_self, w_neigh, bias):
    return pl.pallas_call(
        project_kernel,
        out_shape=jax.ShapeDtypeStruct(mean.shape, mean.dtype),
        name="project",
    )(features, mean, w_self, w_neigh, bias[:, None])


def shards(
    features,
    w_self,
    w_neigh,
    bias,
    hub_pick,
    halo_send,
    tile_dst,
    tile_src,
    tile_edges,
    tile_count,
    edge_src,
    edge_dst,
):
    rows, nodes = features.shape
    parts = lax.axis_size("feat")
    count = lax.axis_size("graph")
    halo = halo_send.shape[0] // 2
    hub_local, outgoing = pick_blocks(features, hub_pick, halo_send)

    along_z = [[X * z + x for z in range(r, Z, STRIDE)] for r in range(STRIDE) for x in range(X)]
    nearby = [
        [X * (z + r) + x for r in range(STRIDE) for x in range(X)] for z in range(0, Z, STRIDE)
    ]
    column = lax.all_gather(hub_local, "graph", axis_index_groups=along_z)
    spread = jnp.broadcast_to(column[None], (X * STRIDE, *column.shape))
    hub_rows = lax.all_to_all(spread, "graph", 0, 0, axis_index_groups=nearby)
    hub_rows = hub_rows.reshape(-1, rows, BLOCK)

    forward = [(i, (i + 1) % count) for i in range(count)]
    backward = [(target, source) for source, target in forward]
    halo_low = lax.ppermute(outgoing[halo:], "graph", forward)
    halo_high = lax.ppermute(outgoing[:halo], "graph", backward)

    means = neighbour_mean(
        features, hub_rows, halo_low, halo_high, tile_dst, tile_src, tile_edges, tile_count, edge_src, edge_dst, parts
    )
    every = lax.all_gather(features, "feat", axis=0, tiled=True)
    width = nodes // parts
    inputs = lax.dynamic_slice_in_dim(every, lax.axis_index("feat") * width, width, 1)
    means = lax.all_to_all(means, "feat", 0, 0).reshape(parts * rows, width)
    updated = project(inputs, means, w_self, w_neigh, bias).reshape(parts, rows, width)
    updated = lax.all_to_all(updated, "feat", 0, 0)
    return jnp.transpose(updated, (1, 0, 2)).reshape(rows, nodes)


def solution(mesh):
    in_specs = (
        P("feat", "graph"),
        P(),
        P(),
        P(),
        P("graph"),
        P("graph"),
        P("graph"),
        P("graph"),
        P("graph"),
        P("graph"),
        P("graph", None),
        P("graph", None),
    )
    out_specs = P("feat", "graph")
    return jax.shard_map(shards, mesh=mesh, in_specs=in_specs, out_specs=out_specs, check_vma=False)
```

```python
import jax
import jax.numpy as jnp
from jax import lax
from jax.experimental import pallas as pl
from jax.experimental.pallas import tpu as pltpu
from jax.sharding import PartitionSpec as P

BLOCK = 128
GROUP = 8
Z, X = 32, 4
STRIDE = 2


def pick_kernel(hub_pick, halo_send, features, hub_out, halo_out):
    def copy(out, picks):
        for i in range(out.shape[0]):
            start = pl.multiple_of(picks[i] * BLOCK, BLOCK)
            out[i] = features[:, pl.ds(start, BLOCK)]

    copy(hub_out, hub_pick)
    copy(halo_out, halo_send)


def pick_blocks(features, hub_pick, halo_send):
    rows = features.shape[0]
    smem = pl.BlockSpec(memory_space=pltpu.SMEM)
    vmem = pl.BlockSpec(memory_space=pltpu.VMEM)
    return pl.pallas_call(
        pick_kernel,
        out_shape=[
            jax.ShapeDtypeStruct((hub_pick.shape[0], rows, BLOCK), features.dtype),
            jax.ShapeDtypeStruct((halo_send.shape[0], rows, BLOCK), features.dtype),
        ],
        in_specs=[smem, smem, vmem],
        out_specs=[vmem, vmem],
        name="pick_blocks",
    )(hub_pick, halo_send, features)


def table_row(slot, own, hubs):
    hub = slot - own
    group = X * STRIDE
    owner = hub >> 1
    place = ((owner & (group - 1)) * (hubs // group)) + ((owner // group) << 1) + (hub & 1)
    return jnp.where((hub >= 0) & (hub < hubs), own + place, slot)


def mean_kernel(
    tile_dst,
    tile_src,
    tile_edges,
    tile_count,
    features,
    edge_src,
    edge_dst,
    hub_rows,
    halo_low,
    halo_high,
    shares,
    table,
    sums,
    sems,
):
    rows = features.shape[0]
    own = features.shape[1] // BLOCK
    hubs = hub_rows.shape[0]
    halo = halo_low.shape[0]
    copies = [
        pltpu.make_async_copy(hub_rows, table.at[pl.ds(own, hubs)], sems.at[0]),
        pltpu.make_async_copy(halo_low, table.at[pl.ds(own + hubs, halo)], sems.at[1]),
        pltpu.make_async_copy(halo_high, table.at[pl.ds(own + hubs + halo, halo)], sems.at[2]),
    ]
    for copy in copies:
        copy.start()
    for b in range(own):
        table[b] = features[:, b * BLOCK : (b + 1) * BLOCK]
        sums[b] = jnp.zeros(sums.shape[1:], jnp.float32)
    for copy in copies:
        copy.wait()

    count = tile_count[0]
    lane = lax.broadcasted_iota(jnp.int32, (8, BLOCK), 1)
    node = lax.broadcasted_iota(jnp.int32, (BLOCK, BLOCK), 0)
    ones = jnp.ones((sums.shape[1] - rows, BLOCK), jnp.float32)

    @pl.loop(0, (count + GROUP - 1) // GROUP)
    def _(step):
        first = pl.multiple_of(step * GROUP, GROUP)
        sources = edge_src[pl.ds(first, GROUP), :]
        targets = edge_dst[pl.ds(first, GROUP), :]
        parts = []
        for i in range(GROUP):
            tile = first + i
            live = jnp.where(tile < count, tile_edges[tile], 0)
            block = table[table_row(tile_src[tile], own, hubs)].astype(jnp.float32)
            index = jnp.broadcast_to(sources[i : i + 1], (8, BLOCK))
            values = [
                jnp.take_along_axis(block[r : r + 8], index, axis=1, mode="promise_in_bounds")
                for r in range(0, rows, 8)
            ]
            left = jnp.concatenate(values + [ones], axis=0).astype(jnp.bfloat16)
            target = jnp.where(lane < live, jnp.broadcast_to(targets[i : i + 1], (8, BLOCK)), -1)
            hits = node == jnp.broadcast_to(target[:1], (BLOCK, BLOCK))
            right = jnp.where(hits, 1.0, 0.0).astype(jnp.bfloat16)
            parts.append(
                lax.dot_general(
                    left, right, (((1,), (1,)), ((), ())), preferred_element_type=jnp.float32
                )
            )
        for i in range(GROUP):
            place = tile_dst[first + i]
            sums[place] = sums[place] + parts[i]

    per = own // shares.shape[0]
    for b in range(own):
        total = sums[b]
        degree = jnp.maximum(total[rows : rows + 8], 1.0)
        mean = jnp.concatenate([total[r : r + 8] / degree for r in range(0, rows, 8)], axis=0)
        at = (b % per) * BLOCK
        shares[b // per, :rows, at : at + BLOCK] = table[b]
        shares[b // per, rows:, at : at + BLOCK] = mean.astype(shares.dtype)


def neighbour_mean(
    features, hub_rows, halo_low, halo_high, tile_dst, tile_src, tile_edges, tile_count, edge_src, edge_dst, parts
):
    rows, nodes = features.shape
    own = nodes // BLOCK
    slots = own + hub_rows.shape[0] + 2 * halo_low.shape[0]
    smem = pl.BlockSpec(memory_space=pltpu.SMEM)
    vmem = pl.BlockSpec(memory_space=pltpu.VMEM)
    anywhere = pl.BlockSpec(memory_space=pl.ANY)
    return pl.pallas_call(
        mean_kernel,
        out_shape=jax.ShapeDtypeStruct((parts, 2 * rows, nodes // parts), features.dtype),
        in_specs=[smem] * 4 + [vmem] * 3 + [anywhere] * 3,
        out_specs=vmem,
        scratch_shapes=[
            pltpu.VMEM((slots, rows, BLOCK), features.dtype),
            pltpu.VMEM((own, 2 * rows, BLOCK), jnp.float32),
            pltpu.SemaphoreType.DMA((3,)),
        ],
        compiler_params=pltpu.CompilerParams(vmem_limit_bytes=32 * 1024 * 1024),
        name="neighbour_mean",
    )(tile_dst, tile_src, tile_edges, tile_count, features, edge_src, edge_dst, hub_rows, halo_low, halo_high)


def project_kernel(shares, w_self, w_neigh, bias, out):
    parts, rows, _ = out.shape

    def whole(first):
        return jnp.concatenate([shares[p, first : first + rows] for p in range(parts)], axis=0)

    total = jnp.dot(w_self[...], whole(0), preferred_element_type=jnp.float32) + jnp.dot(
        w_neigh[...], whole(rows), preferred_element_type=jnp.float32
    )
    updated = jnp.maximum(total + bias[...], 0.0).astype(out.dtype)
    for p in range(parts):
        out[p] = updated[p * rows : (p + 1) * rows]


def project(shares, w_self, w_neigh, bias):
    parts, rows, width = shares.shape
    return pl.pallas_call(
        project_kernel,
        out_shape=jax.ShapeDtypeStruct((parts, rows // 2, width), shares.dtype),
        name="project",
    )(shares, w_self, w_neigh, bias[:, None])


def shards(
    features,
    w_self,
    w_neigh,
    bias,
    hub_pick,
    halo_send,
    tile_dst,
    tile_src,
    tile_edges,
    tile_count,
    edge_src,
    edge_dst,
):
    rows, nodes = features.shape
    parts = lax.axis_size("feat")
    count = lax.axis_size("graph")
    halo = halo_send.shape[0] // 2
    hub_local, outgoing = pick_blocks(features, hub_pick, halo_send)

    along_z = [[X * z + x for z in range(r, Z, STRIDE)] for r in range(STRIDE) for x in range(X)]
    nearby = [
        [X * (z + r) + x for r in range(STRIDE) for x in range(X)] for z in range(0, Z, STRIDE)
    ]
    column = lax.all_gather(hub_local, "graph", axis_index_groups=along_z)
    spread = jnp.broadcast_to(column[None], (X * STRIDE, *column.shape))
    hub_rows = lax.all_to_all(spread, "graph", 0, 0, axis_index_groups=nearby)
    hub_rows = hub_rows.reshape(-1, rows, BLOCK)

    forward = [(i, (i + 1) % count) for i in range(count)]
    backward = [(target, source) for source, target in forward]
    halo_low = lax.ppermute(outgoing[halo:], "graph", forward)
    halo_high = lax.ppermute(outgoing[:halo], "graph", backward)

    shares = neighbour_mean(
        features, hub_rows, halo_low, halo_high, tile_dst, tile_src, tile_edges, tile_count, edge_src, edge_dst, parts
    )
    shares = lax.all_to_all(shares, "feat", 0, 0)
    updated = lax.all_to_all(project(shares, w_self, w_neigh, bias), "feat", 0, 0)
    return jnp.transpose(updated, (1, 0, 2)).reshape(rows, nodes)


def solution(mesh):
    in_specs = (
        P("feat", "graph"),
        P(),
        P(),
        P(),
        P("graph"),
        P("graph"),
        P("graph"),
        P("graph"),
        P("graph"),
        P("graph"),
        P("graph", None),
        P("graph", None),
    )
    out_specs = P("feat", "graph")
    return jax.shard_map(shards, mesh=mesh, in_specs=in_specs, out_specs=out_specs, check_vma=False)
```

```python
import jax
import jax.numpy as jnp
from jax import lax
from jax.experimental import pallas as pl
from jax.experimental.pallas import tpu as pltpu
from jax.sharding import PartitionSpec as P

BLOCK = 128
GROUP = 32
Z, X = 32, 4
STRIDE = 2


def pick_kernel(hub_pick, halo_send, features, hub_out, halo_out):
    def copy(out, picks):
        for i in range(out.shape[0]):
            start = pl.multiple_of(picks[i] * BLOCK, BLOCK)
            out[i] = features[:, pl.ds(start, BLOCK)]

    copy(hub_out, hub_pick)
    copy(halo_out, halo_send)


def pick_blocks(features, hub_pick, halo_send):
    rows = features.shape[0]
    smem = pl.BlockSpec(memory_space=pltpu.SMEM)
    vmem = pl.BlockSpec(memory_space=pltpu.VMEM)
    return pl.pallas_call(
        pick_kernel,
        out_shape=[
            jax.ShapeDtypeStruct((hub_pick.shape[0], rows, BLOCK), features.dtype),
            jax.ShapeDtypeStruct((halo_send.shape[0], rows, BLOCK), features.dtype),
        ],
        in_specs=[smem, smem, vmem],
        out_specs=[vmem, vmem],
        name="pick_blocks",
    )(hub_pick, halo_send, features)


def hub_row(hub, hubs):
    group = X * STRIDE
    owner = hub >> 1
    return (owner & (group - 1)) * (hubs // group) + ((owner // group) << 1) + (hub & 1)


def mean_kernel(
    tile_dst,
    tile_src,
    tile_edges,
    tile_count,
    features,
    edge_src,
    edge_dst,
    hub_rows,
    halo_low,
    halo_high,
    shares,
    table,
    sums,
):
    rows = features.shape[0]
    own = features.shape[1] // BLOCK
    hubs = hub_rows.shape[0]
    halo = halo_low.shape[0]
    for b in range(own):
        table[b] = features[:, b * BLOCK : (b + 1) * BLOCK]
        sums[b] = jnp.zeros(sums.shape[1:], jnp.float32)
    for b in range(halo):
        table[own + b] = halo_low[b]
        table[own + halo + b] = halo_high[b]

    count = tile_count[0]
    lane = lax.broadcasted_iota(jnp.int32, (8, BLOCK), 1)
    node = lax.broadcasted_iota(jnp.int32, (BLOCK, BLOCK), 0).astype(jnp.bfloat16)
    one, zero = jnp.ones((), jnp.bfloat16), jnp.zeros((), jnp.bfloat16)
    ones = jnp.ones((rows, BLOCK), jnp.bfloat16)
    blank = jnp.zeros((2 * rows, BLOCK), jnp.bfloat16)

    @pl.loop(0, (count + GROUP - 1) // GROUP)
    def _(step):
        first = pl.multiple_of(step * GROUP, GROUP)
        sources = edge_src[pl.ds(first, GROUP), :]
        targets = edge_dst[pl.ds(first, GROUP), :]
        lefts, rights, parts = [], [], []
        for i in range(GROUP):
            tile = first + i
            slot = tile_src[tile]
            hub = slot - own
            is_hub = (hub >= 0) & (hub < hubs)
            near = table[jnp.where(is_hub, 0, jnp.where(hub < 0, slot, slot - hubs))]
            far = hub_rows[jnp.where(is_hub, hub_row(hub, hubs), 0)]
            block = jnp.where(is_hub, far, near).astype(jnp.float32)
            index = jnp.broadcast_to(sources[i : i + 1], (8, BLOCK))
            values = [
                jnp.take_along_axis(block[r : r + 8], index, axis=1, mode="promise_in_bounds")
                for r in range(0, rows, 8)
            ]
            values = jnp.concatenate(values, axis=0).astype(jnp.bfloat16)
            lefts.append(jnp.concatenate([values, ones], axis=0))
            live = jnp.where(tile < count, tile_edges[tile], 0)
            target = jnp.where(lane < live, jnp.broadcast_to(targets[i : i + 1], (8, BLOCK)), -1)
            hits = node == jnp.broadcast_to(target[:1].astype(jnp.bfloat16), (BLOCK, BLOCK))
            rights.append(jnp.where(hits, one, zero))
        for i in range(0, GROUP, 2):
            left = jnp.concatenate(
                [
                    jnp.concatenate([lefts[i], blank], axis=1),
                    jnp.concatenate([blank, lefts[i + 1]], axis=1),
                ],
                axis=0,
            )
            right = jnp.concatenate([rights[i], rights[i + 1]], axis=1)
            both = lax.dot_general(
                left, right, (((1,), (1,)), ((), ())), preferred_element_type=jnp.float32
            )
            parts.append(both[: rows + 8])
            parts.append(both[2 * rows : 3 * rows + 8])
        for i in range(GROUP):
            place = tile_dst[first + i]
            sums[place] = sums[place] + parts[i]

    per = own // shares.shape[0]
    for b in range(own):
        total = sums[b]
        degree = jnp.maximum(total[rows : rows + 8], 1.0)
        mean = jnp.concatenate([total[r : r + 8] / degree for r in range(0, rows, 8)], axis=0)
        at = (b % per) * BLOCK
        shares[b // per, :rows, at : at + BLOCK] = table[b]
        shares[b // per, rows:, at : at + BLOCK] = mean.astype(shares.dtype)


def neighbour_mean(
    features, hub_rows, halo_low, halo_high, tile_dst, tile_src, tile_edges, tile_count, edge_src, edge_dst, parts
):
    rows, nodes = features.shape
    own = nodes // BLOCK
    smem = pl.BlockSpec(memory_space=pltpu.SMEM)
    vmem = pl.BlockSpec(memory_space=pltpu.VMEM)
    return pl.pallas_call(
        mean_kernel,
        out_shape=jax.ShapeDtypeStruct((parts, 2 * rows, nodes // parts), features.dtype),
        in_specs=[smem] * 4 + [vmem] * 6,
        out_specs=vmem,
        scratch_shapes=[
            pltpu.VMEM((own + 2 * halo_low.shape[0], rows, BLOCK), features.dtype),
            pltpu.VMEM((own, rows + 8, BLOCK), jnp.float32),
        ],
        compiler_params=pltpu.CompilerParams(vmem_limit_bytes=32 * 1024 * 1024),
        name="neighbour_mean",
    )(tile_dst, tile_src, tile_edges, tile_count, features, edge_src, edge_dst, hub_rows, halo_low, halo_high)


def project_kernel(shares, w_self, w_neigh, bias, out):
    parts, rows, _ = out.shape

    def whole(first):
        return jnp.concatenate([shares[p, first : first + rows] for p in range(parts)], axis=0)

    total = jnp.dot(w_self[...], whole(0), preferred_element_type=jnp.float32) + jnp.dot(
        w_neigh[...], whole(rows), preferred_element_type=jnp.float32
    )
    width = total.shape[0]
    column = jnp.transpose(jnp.broadcast_to(bias[...], (width, width)))
    total = total + jnp.concatenate([column] * (total.shape[1] // width), axis=1)
    updated = jnp.maximum(total, 0.0).astype(out.dtype)
    for p in range(parts):
        out[p] = updated[p * rows : (p + 1) * rows]


def project(shares, w_self, w_neigh, bias):
    parts, rows, width = shares.shape
    vmem = pl.BlockSpec(memory_space=pltpu.VMEM)
    return pl.pallas_call(
        project_kernel,
        out_shape=jax.ShapeDtypeStruct((parts, rows // 2, width), shares.dtype),
        in_specs=[vmem] * 4,
        out_specs=vmem,
        name="project",
    )(shares, w_self, w_neigh, bias[None, :])


def shards(
    features,
    w_self,
    w_neigh,
    bias,
    hub_pick,
    halo_send,
    tile_dst,
    tile_src,
    tile_edges,
    tile_count,
    edge_src,
    edge_dst,
):
    rows, nodes = features.shape
    parts = lax.axis_size("feat")
    count = lax.axis_size("graph")
    halo = halo_send.shape[0] // 2
    hub_local, outgoing = pick_blocks(features, hub_pick, halo_send)

    along_z = [[X * z + x for z in range(r, Z, STRIDE)] for r in range(STRIDE) for x in range(X)]
    nearby = [
        [X * (z + r) + x for r in range(STRIDE) for x in range(X)] for z in range(0, Z, STRIDE)
    ]
    column = lax.all_gather(hub_local, "graph", axis_index_groups=along_z)
    spread = jnp.broadcast_to(column[None], (X * STRIDE, *column.shape))
    hub_rows = lax.all_to_all(spread, "graph", 0, 0, axis_index_groups=nearby)
    hub_rows = hub_rows.reshape(-1, rows, BLOCK)

    forward = [(i, (i + 1) % count) for i in range(count)]
    backward = [(target, source) for source, target in forward]
    halo_low = lax.ppermute(outgoing[halo:], "graph", forward)
    halo_high = lax.ppermute(outgoing[:halo], "graph", backward)

    shares = neighbour_mean(
        features, hub_rows, halo_low, halo_high, tile_dst, tile_src, tile_edges, tile_count, edge_src, edge_dst, parts
    )
    shares = lax.all_to_all(shares, "feat", 0, 0)
    updated = lax.all_to_all(project(shares, w_self, w_neigh, bias), "feat", 0, 0)
    return jnp.transpose(updated, (1, 0, 2)).reshape(rows, nodes)


def solution(mesh):
    in_specs = (
        P("feat", "graph"),
        P(),
        P(),
        P(),
        P("graph"),
        P("graph"),
        P("graph"),
        P("graph"),
        P("graph"),
        P("graph"),
        P("graph", None),
        P("graph", None),
    )
    out_specs = P("feat", "graph")
    return jax.shard_map(shards, mesh=mesh, in_specs=in_specs, out_specs=out_specs, check_vma=False)
```

```python
import jax
import jax.numpy as jnp
from jax import lax
from jax.experimental import pallas as pl
from jax.experimental.pallas import tpu as pltpu
from jax.sharding import PartitionSpec as P

BLOCK = 128
GROUP = 64
Z, X = 32, 4
STRIDE = 2


def pick_kernel(hub_pick, halo_send, features, hub_out, before_out, after_out):
    def copy(out, picks, first):
        for i in range(out.shape[0]):
            start = pl.multiple_of(picks[first + i] * BLOCK, BLOCK)
            out[i] = features[:, pl.ds(start, BLOCK)]

    copy(hub_out, hub_pick, 0)
    copy(before_out, halo_send, 0)
    copy(after_out, halo_send, before_out.shape[0])


def pick_blocks(features, hub_pick, halo_send):
    rows = features.shape[0]
    smem = pl.BlockSpec(memory_space=pltpu.SMEM)
    vmem = pl.BlockSpec(memory_space=pltpu.VMEM)
    return pl.pallas_call(
        pick_kernel,
        out_shape=[
            jax.ShapeDtypeStruct((hub_pick.shape[0], rows, BLOCK), features.dtype),
            jax.ShapeDtypeStruct((halo_send.shape[0] // 2, rows, BLOCK), features.dtype),
            jax.ShapeDtypeStruct((halo_send.shape[0] // 2, rows, BLOCK), features.dtype),
        ],
        in_specs=[smem, smem, vmem],
        out_specs=[vmem] * 3,
        name="pick_blocks",
    )(hub_pick, halo_send, features)


def hub_row(hub, hubs):
    group = X * STRIDE
    owner = hub >> 1
    return (owner & (group - 1)) * (hubs // group) + ((owner // group) << 1) + (hub & 1)


def mean_kernel(
    plan,
    features,
    edge_src,
    edge_dst,
    hub_rows,
    halo_low,
    halo_high,
    shares,
    table,
    sums,
):
    rows = features.shape[0]
    own = features.shape[1] // BLOCK
    halo = halo_low.shape[0]
    for b in range(own):
        table[b] = features[:, b * BLOCK : (b + 1) * BLOCK]
        sums[b] = jnp.zeros(sums.shape[1:], jnp.float32)
    for b in range(halo):
        table[own + b] = halo_low[b]
        table[own + halo + b] = halo_high[b]

    slots = edge_src.shape[0]
    tile_dst, tile_near, tile_far, tile_live = (plan.at[pl.ds(i * slots, slots)] for i in range(4))
    count = plan[4 * slots]
    lane = lax.broadcasted_iota(jnp.int32, (8, BLOCK), 1)
    node = lax.broadcasted_iota(jnp.int32, (BLOCK, BLOCK), 0).astype(jnp.bfloat16)
    one, zero = jnp.ones((), jnp.bfloat16), jnp.zeros((), jnp.bfloat16)
    blank = jnp.zeros((rows, BLOCK), jnp.bfloat16)
    upper = lax.broadcasted_iota(jnp.int32, (16, 2 * BLOCK), 0) < 8
    first_tile = lax.broadcasted_iota(jnp.int32, (16, 2 * BLOCK), 1) < BLOCK
    ones = jnp.where(upper == first_tile, 1.0, 0.0).astype(jnp.bfloat16)

    @pl.loop(0, (count + GROUP - 1) // GROUP)
    def _(step):
        first = pl.multiple_of(step * GROUP, GROUP)
        sources = edge_src[pl.ds(first, GROUP), :]
        targets = edge_dst[pl.ds(first, GROUP), :]
        lefts, rights, parts = [], [], []
        for i in range(GROUP):
            tile = first + i
            far = tile_far[tile]
            block = jnp.where(far >= 0, hub_rows[jnp.maximum(far, 0)], table[tile_near[tile]])
            block = block.astype(jnp.float32)
            index = jnp.broadcast_to(sources[i : i + 1], (8, BLOCK))
            values = [
                jnp.take_along_axis(block[r : r + 8], index, axis=1, mode="promise_in_bounds")
                for r in range(0, rows, 8)
            ]
            lefts.append(jnp.concatenate(values, axis=0).astype(jnp.bfloat16))
            target = jnp.where(lane < tile_live[tile], jnp.broadcast_to(targets[i : i + 1], (8, BLOCK)), -1)
            hits = node == jnp.broadcast_to(target[:1].astype(jnp.bfloat16), (BLOCK, BLOCK))
            rights.append(jnp.where(hits, one, zero))
        for i in range(0, GROUP, 2):
            left = jnp.concatenate(
                [
                    jnp.concatenate([lefts[i], blank], axis=1),
                    jnp.concatenate([blank, lefts[i + 1]], axis=1),
                    ones,
                ],
                axis=0,
            )
            right = jnp.concatenate([rights[i], rights[i + 1]], axis=1)
            both = lax.dot_general(
                left, right, (((1,), (1,)), ((), ())), preferred_element_type=jnp.float32
            )
            for k in range(2):
                values = both[k * rows : (k + 1) * rows]
                degrees = both[2 * rows + 8 * k : 2 * rows + 8 * (k + 1)]
                parts.append(jnp.concatenate([values, degrees], axis=0))
        for i in range(GROUP):
            place = tile_dst[first + i]
            sums[place] = sums[place] + parts[i]

    per = own // shares.shape[0]
    for b in range(own):
        total = sums[b]
        degree = jnp.maximum(total[rows : rows + 8], 1.0)
        mean = jnp.concatenate([total[r : r + 8] / degree for r in range(0, rows, 8)], axis=0)
        at = (b % per) * BLOCK
        shares[b // per, :rows, at : at + BLOCK] = table[b]
        shares[b // per, rows:, at : at + BLOCK] = mean.astype(shares.dtype)


def neighbour_mean(
    features, hub_rows, halo_low, halo_high, tile_dst, tile_src, tile_edges, tile_count, edge_src, edge_dst, parts
):
    rows, nodes = features.shape
    own = nodes // BLOCK
    hubs = hub_rows.shape[0]
    hub = tile_src - own
    is_hub = (hub >= 0) & (hub < hubs)
    tile_near = jnp.where(is_hub, 0, jnp.where(hub < 0, tile_src, tile_src - hubs))
    tile_far = jnp.where(is_hub, hub_row(hub, hubs), -1)
    tile_live = jnp.where(jnp.arange(tile_src.shape[0], dtype=jnp.int32) < tile_count[0], tile_edges, 0)
    plan = jnp.concatenate([tile_dst, tile_near, tile_far, tile_live, tile_count])
    smem = pl.BlockSpec(memory_space=pltpu.SMEM)
    vmem = pl.BlockSpec(memory_space=pltpu.VMEM)
    return pl.pallas_call(
        mean_kernel,
        out_shape=jax.ShapeDtypeStruct((parts, 2 * rows, nodes // parts), features.dtype),
        in_specs=[smem] + [vmem] * 6,
        out_specs=vmem,
        scratch_shapes=[
            pltpu.VMEM((own + 2 * halo_low.shape[0], rows, BLOCK), features.dtype),
            pltpu.VMEM((own, rows + 8, BLOCK), jnp.float32),
        ],
        compiler_params=pltpu.CompilerParams(vmem_limit_bytes=32 * 1024 * 1024),
        name="neighbour_mean",
    )(plan, features, edge_src, edge_dst, hub_rows, halo_low, halo_high)


def project_kernel(shares, w_self, w_neigh, bias, out):
    parts, rows, _ = out.shape

    def whole(first):
        return jnp.concatenate([shares[p, first : first + rows] for p in range(parts)], axis=0)

    total = jnp.dot(w_self[...], whole(0), preferred_element_type=jnp.float32) + jnp.dot(
        w_neigh[...], whole(rows), preferred_element_type=jnp.float32
    )
    width = total.shape[0]
    column = jnp.transpose(jnp.broadcast_to(bias[...], (width, width)))
    total = total + jnp.concatenate([column] * (total.shape[1] // width), axis=1)
    updated = jnp.maximum(total, 0.0).astype(out.dtype)
    for p in range(parts):
        out[p] = updated[p * rows : (p + 1) * rows]


def project(shares, w_self, w_neigh, bias):
    parts, rows, width = shares.shape
    vmem = pl.BlockSpec(memory_space=pltpu.VMEM)
    return pl.pallas_call(
        project_kernel,
        out_shape=jax.ShapeDtypeStruct((parts, rows // 2, width), shares.dtype),
        in_specs=[vmem] * 4,
        out_specs=vmem,
        name="project",
    )(shares, w_self, w_neigh, bias[None, :])


def shards(
    features,
    w_self,
    w_neigh,
    bias,
    hub_pick,
    halo_send,
    tile_dst,
    tile_src,
    tile_edges,
    tile_count,
    edge_src,
    edge_dst,
):
    rows, nodes = features.shape
    parts = lax.axis_size("feat")
    count = lax.axis_size("graph")
    hub_local, to_previous, to_next = pick_blocks(features, hub_pick, halo_send)

    along_z = [[X * z + x for z in range(r, Z, STRIDE)] for r in range(STRIDE) for x in range(X)]
    nearby = [
        [X * (z + r) + x for r in range(STRIDE) for x in range(X)] for z in range(0, Z, STRIDE)
    ]
    column = lax.all_gather(hub_local, "graph", axis_index_groups=along_z)
    column, tile_src, tile_edges = lax.optimization_barrier((column, tile_src, tile_edges))
    spread = jnp.broadcast_to(column[None], (X * STRIDE, *column.shape))
    hub_rows = lax.all_to_all(spread, "graph", 0, 0, axis_index_groups=nearby)
    hub_rows = hub_rows.reshape(-1, rows, BLOCK)

    forward = [(i, (i + 1) % count) for i in range(count)]
    backward = [(target, source) for source, target in forward]
    halo_low = lax.ppermute(to_next, "graph", forward)
    halo_high = lax.ppermute(to_previous, "graph", backward)

    shares = neighbour_mean(
        features, hub_rows, halo_low, halo_high, tile_dst, tile_src, tile_edges, tile_count, edge_src, edge_dst, parts
    )
    shares = lax.all_to_all(shares, "feat", 0, 0)
    updated = lax.all_to_all(project(shares, w_self, w_neigh, bias), "feat", 0, 0)
    return jnp.transpose(updated, (1, 0, 2)).reshape(rows, nodes)


def solution(mesh):
    in_specs = (
        P("feat", "graph"),
        P(),
        P(),
        P(),
        P("graph"),
        P("graph"),
        P("graph"),
        P("graph"),
        P("graph"),
        P("graph"),
        P("graph", None),
        P("graph", None),
    )
    out_specs = P("feat", "graph")
    return jax.shard_map(shards, mesh=mesh, in_specs=in_specs, out_specs=out_specs, check_vma=False)
```

```python
import jax
import jax.numpy as jnp
from jax import lax
from jax.experimental import pallas as pl
from jax.experimental.pallas import tpu as pltpu
from jax.sharding import PartitionSpec as P

BLOCK = 128
GROUP = 64
Z, X = 32, 4
STRIDE = 2


def pick_kernel(hub_pick, halo_send, features, hub_out, before_out, after_out):
    def copy(out, picks, first):
        for i in range(out.shape[0]):
            start = pl.multiple_of(picks[first + i] * BLOCK, BLOCK)
            out[i] = features[:, pl.ds(start, BLOCK)]

    copy(hub_out, hub_pick, 0)
    copy(before_out, halo_send, 0)
    copy(after_out, halo_send, before_out.shape[0])


def pick_blocks(features, hub_pick, halo_send):
    rows = features.shape[0]
    smem = pl.BlockSpec(memory_space=pltpu.SMEM)
    vmem = pl.BlockSpec(memory_space=pltpu.VMEM)
    return pl.pallas_call(
        pick_kernel,
        out_shape=[
            jax.ShapeDtypeStruct((hub_pick.shape[0], rows, BLOCK), features.dtype),
            jax.ShapeDtypeStruct((halo_send.shape[0] // 2, rows, BLOCK), features.dtype),
            jax.ShapeDtypeStruct((halo_send.shape[0] // 2, rows, BLOCK), features.dtype),
        ],
        in_specs=[smem, smem, vmem],
        out_specs=[vmem] * 3,
        name="pick_blocks",
    )(hub_pick, halo_send, features)


def hub_row(hub, hubs):
    group = X * STRIDE
    owner = hub >> 1
    return (owner & (group - 1)) * (hubs // group) + ((owner // group) << 1) + (hub & 1)


def mean_kernel(
    plan,
    features,
    edge_src,
    edge_dst,
    hub_rows,
    halo_low,
    halo_high,
    shares,
    table,
    sums,
):
    rows = features.shape[0]
    own = features.shape[1] // BLOCK
    halo = halo_low.shape[0]
    for b in range(own):
        table[b] = features[:, b * BLOCK : (b + 1) * BLOCK]
        sums[b] = jnp.zeros(sums.shape[1:], jnp.float32)
    for b in range(halo):
        table[own + b] = halo_low[b]
        table[own + halo + b] = halo_high[b]

    slots = edge_src.shape[0]
    tile_dst, tile_near, tile_far, tile_live = (plan.at[pl.ds(i * slots, slots)] for i in range(4))
    count = plan[4 * slots]
    lane = lax.broadcasted_iota(jnp.int32, (8, BLOCK), 1)
    node = lax.broadcasted_iota(jnp.int32, (BLOCK, BLOCK), 0).astype(jnp.bfloat16)
    one, zero = jnp.ones((), jnp.bfloat16), jnp.zeros((), jnp.bfloat16)
    blank = jnp.zeros((rows, BLOCK), jnp.bfloat16)
    upper = lax.broadcasted_iota(jnp.int32, (16, 2 * BLOCK), 0) < 8
    first_tile = lax.broadcasted_iota(jnp.int32, (16, 2 * BLOCK), 1) < BLOCK
    ones = jnp.where(upper == first_tile, 1.0, 0.0).astype(jnp.bfloat16)

    @pl.loop(0, (count + GROUP - 1) // GROUP)
    def _(step):
        first = pl.multiple_of(step * GROUP, GROUP)
        sources = edge_src[pl.ds(first, GROUP), :]
        targets = edge_dst[pl.ds(first, GROUP), :]
        lefts, rights, parts = [], [], []
        for i in range(GROUP):
            tile = first + i
            far = tile_far[tile]
            block = jnp.where(far >= 0, hub_rows[jnp.maximum(far, 0)], table[tile_near[tile]])
            block = block.astype(jnp.float32)
            index = jnp.broadcast_to(sources[i : i + 1], (8, BLOCK))
            values = [
                jnp.take_along_axis(block[r : r + 8], index, axis=1, mode="promise_in_bounds")
                for r in range(0, rows, 8)
            ]
            lefts.append(jnp.concatenate(values, axis=0).astype(jnp.bfloat16))
            target = jnp.where(lane < tile_live[tile], jnp.broadcast_to(targets[i : i + 1], (8, BLOCK)), -1)
            hits = node == jnp.broadcast_to(target[:1].astype(jnp.bfloat16), (BLOCK, BLOCK))
            rights.append(jnp.where(hits, one, zero))
        for i in range(0, GROUP, 2):
            left = jnp.concatenate(
                [
                    jnp.concatenate([lefts[i], blank], axis=1),
                    jnp.concatenate([blank, lefts[i + 1]], axis=1),
                    ones,
                ],
                axis=0,
            )
            right = jnp.concatenate([rights[i], rights[i + 1]], axis=1)
            both = lax.dot_general(
                left, right, (((1,), (1,)), ((), ())), preferred_element_type=jnp.float32
            )
            for k in range(2):
                values = both[k * rows : (k + 1) * rows]
                degrees = both[2 * rows + 8 * k : 2 * rows + 8 * (k + 1)]
                parts.append(jnp.concatenate([values, degrees], axis=0))
        for i in range(GROUP):
            place = tile_dst[first + i]
            sums[place] = sums[place] + parts[i]

    per = own // shares.shape[0]
    for b in range(own):
        total = sums[b]
        degree = jnp.maximum(total[rows : rows + 8], 1.0)
        mean = jnp.concatenate([total[r : r + 8] / degree for r in range(0, rows, 8)], axis=0)
        at = (b % per) * BLOCK
        shares[b // per, :rows, at : at + BLOCK] = table[b]
        shares[b // per, rows:, at : at + BLOCK] = mean.astype(shares.dtype)


def neighbour_mean(
    features, hub_rows, halo_low, halo_high, tile_dst, tile_src, tile_edges, tile_count, edge_src, edge_dst, parts
):
    rows, nodes = features.shape
    own = nodes // BLOCK
    hubs = hub_rows.shape[0]
    hub = tile_src - own
    is_hub = (hub >= 0) & (hub < hubs)
    tile_near = jnp.where(is_hub, 0, jnp.where(hub < 0, tile_src, tile_src - hubs))
    tile_far = jnp.where(is_hub, hub_row(hub, hubs), -1)
    tile_live = jnp.where(jnp.arange(tile_src.shape[0], dtype=jnp.int32) < tile_count[0], tile_edges, 0)
    plan = jnp.concatenate([tile_dst, tile_near, tile_far, tile_live, tile_count])
    smem = pl.BlockSpec(memory_space=pltpu.SMEM)
    vmem = pl.BlockSpec(memory_space=pltpu.VMEM)
    return pl.pallas_call(
        mean_kernel,
        out_shape=jax.ShapeDtypeStruct((parts, 2 * rows, nodes // parts), features.dtype),
        in_specs=[smem] + [vmem] * 6,
        out_specs=vmem,
        scratch_shapes=[
            pltpu.VMEM((own + 2 * halo_low.shape[0], rows, BLOCK), features.dtype),
            pltpu.VMEM((own, rows + 8, BLOCK), jnp.float32),
        ],
        compiler_params=pltpu.CompilerParams(vmem_limit_bytes=32 * 1024 * 1024),
        name="neighbour_mean",
    )(plan, features, edge_src, edge_dst, hub_rows, halo_low, halo_high)


def project(shares, weights, bias):
    parts, rows, width = shares.shape
    total = jnp.dot(weights, shares.reshape(parts * rows, width), preferred_element_type=jnp.float32)
    updated = jnp.maximum(total + bias[:, None], 0.0).astype(shares.dtype)
    return updated.reshape(parts, rows // 2, width)


def shards(
    features,
    w_self,
    w_neigh,
    bias,
    hub_pick,
    halo_send,
    tile_dst,
    tile_src,
    tile_edges,
    tile_count,
    edge_src,
    edge_dst,
):
    rows, nodes = features.shape
    parts = lax.axis_size("feat")
    count = lax.axis_size("graph")
    hub_local, to_previous, to_next = pick_blocks(features, hub_pick, halo_send)

    along_z = [[X * z + x for z in range(r, Z, STRIDE)] for r in range(STRIDE) for x in range(X)]
    nearby = [
        [X * (z + r) + x for r in range(STRIDE) for x in range(X)] for z in range(0, Z, STRIDE)
    ]
    column = lax.all_gather(hub_local, "graph", axis_index_groups=along_z)
    column, tile_src, tile_edges, w_self, w_neigh = lax.optimization_barrier(
        (column, tile_src, tile_edges, w_self, w_neigh)
    )
    weights = jnp.stack(
        [w_self.reshape(-1, parts, rows), w_neigh.reshape(-1, parts, rows)], axis=2
    ).reshape(-1, 2 * parts * rows)
    spread = jnp.broadcast_to(column[None], (X * STRIDE, *column.shape))
    hub_rows = lax.all_to_all(spread, "graph", 0, 0, axis_index_groups=nearby)
    hub_rows = hub_rows.reshape(-1, rows, BLOCK)

    forward = [(i, (i + 1) % count) for i in range(count)]
    backward = [(target, source) for source, target in forward]
    halo_low = lax.ppermute(to_next, "graph", forward)
    halo_high = lax.ppermute(to_previous, "graph", backward)

    hub_rows, weights = lax.optimization_barrier((hub_rows, weights))
    shares = neighbour_mean(
        features, hub_rows, halo_low, halo_high, tile_dst, tile_src, tile_edges, tile_count, edge_src, edge_dst, parts
    )
    shares = lax.all_to_all(shares, "feat", 0, 0)
    updated = lax.all_to_all(project(shares, weights, bias), "feat", 0, 0)
    return jnp.transpose(updated, (1, 0, 2)).reshape(rows, nodes)


def solution(mesh):
    in_specs = (
        P("feat", "graph"),
        P(),
        P(),
        P(),
        P("graph"),
        P("graph"),
        P("graph"),
        P("graph"),
        P("graph"),
        P("graph"),
        P("graph", None),
        P("graph", None),
    )
    out_specs = P("feat", "graph")
    return jax.shard_map(shards, mesh=mesh, in_specs=in_specs, out_specs=out_specs, check_vma=False)
```

```python
import jax
import jax.numpy as jnp
from jax import lax
from jax.experimental import pallas as pl
from jax.experimental.pallas import tpu as pltpu
from jax.sharding import PartitionSpec as P

BLOCK = 128
GROUP = 64
Z, X = 32, 4
STRIDE = 2


def pick_kernel(hub_pick, halo_send, features, hub_out, before_out, after_out):
    def copy(out, picks, first):
        for i in range(out.shape[0]):
            start = pl.multiple_of(picks[first + i] * BLOCK, BLOCK)
            out[i] = features[:, pl.ds(start, BLOCK)]

    copy(hub_out, hub_pick, 0)
    copy(before_out, halo_send, 0)
    copy(after_out, halo_send, before_out.shape[0])


def pick_blocks(features, hub_pick, halo_send):
    rows = features.shape[0]
    smem = pl.BlockSpec(memory_space=pltpu.SMEM)
    vmem = pl.BlockSpec(memory_space=pltpu.VMEM)
    return pl.pallas_call(
        pick_kernel,
        out_shape=[
            jax.ShapeDtypeStruct((hub_pick.shape[0], rows, BLOCK), features.dtype),
            jax.ShapeDtypeStruct((halo_send.shape[0] // 2, rows, BLOCK), features.dtype),
            jax.ShapeDtypeStruct((halo_send.shape[0] // 2, rows, BLOCK), features.dtype),
        ],
        in_specs=[smem, smem, vmem],
        out_specs=[vmem] * 3,
        name="pick_blocks",
    )(hub_pick, halo_send, features)


def hub_row(hub, hubs):
    group = X * STRIDE
    owner = hub >> 1
    return (owner & (group - 1)) * (hubs // group) + ((owner // group) << 1) + (hub & 1)


def mean_kernel(
    plan,
    features,
    edge_src,
    edge_dst,
    hub_rows,
    halo_low,
    halo_high,
    shares,
    table,
    sums,
):
    rows = features.shape[0]
    own = features.shape[1] // BLOCK
    halo = halo_low.shape[0]
    for b in range(own):
        table[b] = features[:, b * BLOCK : (b + 1) * BLOCK]
        sums[b] = jnp.zeros(sums.shape[1:], jnp.float32)
    for b in range(halo):
        table[own + b] = halo_low[b]
        table[own + halo + b] = halo_high[b]

    slots = edge_src.shape[0]
    tile_dst, tile_near, tile_far, tile_live = (plan.at[pl.ds(i * slots, slots)] for i in range(4))
    count = plan[4 * slots]
    lane = lax.broadcasted_iota(jnp.int32, (8, BLOCK), 1)
    node = lax.broadcasted_iota(jnp.int32, (BLOCK, BLOCK), 0).astype(jnp.bfloat16)
    one, zero = jnp.ones((), jnp.bfloat16), jnp.zeros((), jnp.bfloat16)
    blank = jnp.zeros((rows, BLOCK), jnp.bfloat16)
    upper = lax.broadcasted_iota(jnp.int32, (16, 2 * BLOCK), 0) < 8
    first_tile = lax.broadcasted_iota(jnp.int32, (16, 2 * BLOCK), 1) < BLOCK
    ones = jnp.where(upper == first_tile, 1.0, 0.0).astype(jnp.bfloat16)

    @pl.loop(0, (count + GROUP - 1) // GROUP)
    def _(step):
        first = pl.multiple_of(step * GROUP, GROUP)
        sources = edge_src[pl.ds(first, GROUP), :]
        targets = edge_dst[pl.ds(first, GROUP), :]
        lefts, rights, parts = [], [], []
        for i in range(GROUP):
            tile = first + i
            far = tile_far[tile]
            block = jnp.where(far >= 0, hub_rows[jnp.maximum(far, 0)], table[tile_near[tile]])
            block = block.astype(jnp.float32)
            index = jnp.broadcast_to(sources[i : i + 1], (8, BLOCK))
            values = [
                jnp.take_along_axis(block[r : r + 8], index, axis=1, mode="promise_in_bounds")
                for r in range(0, rows, 8)
            ]
            lefts.append(jnp.concatenate(values, axis=0).astype(jnp.bfloat16))
            target = jnp.where(lane < tile_live[tile], jnp.broadcast_to(targets[i : i + 1], (8, BLOCK)), -1)
            hits = node == jnp.broadcast_to(target[:1].astype(jnp.bfloat16), (BLOCK, BLOCK))
            rights.append(jnp.where(hits, one, zero))
        for i in range(0, GROUP, 2):
            left = jnp.concatenate(
                [
                    jnp.concatenate([lefts[i], blank], axis=1),
                    jnp.concatenate([blank, lefts[i + 1]], axis=1),
                    ones,
                ],
                axis=0,
            )
            right = jnp.concatenate([rights[i], rights[i + 1]], axis=1)
            both = lax.dot_general(
                left, right, (((1,), (1,)), ((), ())), preferred_element_type=jnp.float32
            )
            for k in range(2):
                values = both[k * rows : (k + 1) * rows]
                degrees = both[2 * rows + 8 * k : 2 * rows + 8 * (k + 1)]
                parts.append(jnp.concatenate([values, degrees], axis=0))
        for i in range(GROUP):
            place = tile_dst[first + i]
            sums[place] = sums[place] + parts[i]

    per = own // shares.shape[0]
    for b in range(own):
        total = sums[b]
        degree = jnp.maximum(total[rows : rows + 8], 1.0)
        mean = jnp.concatenate([total[r : r + 8] / degree for r in range(0, rows, 8)], axis=0)
        at = (b % per) * BLOCK
        shares[b // per, :, at : at + BLOCK] = mean.astype(shares.dtype)


def neighbour_mean(
    features, hub_rows, halo_low, halo_high, tile_dst, tile_src, tile_edges, tile_count, edge_src, edge_dst, parts
):
    rows, nodes = features.shape
    own = nodes // BLOCK
    hubs = hub_rows.shape[0]
    hub = tile_src - own
    is_hub = (hub >= 0) & (hub < hubs)
    tile_near = jnp.where(is_hub, 0, jnp.where(hub < 0, tile_src, tile_src - hubs))
    tile_far = jnp.where(is_hub, hub_row(hub, hubs), -1)
    tile_live = jnp.where(jnp.arange(tile_src.shape[0], dtype=jnp.int32) < tile_count[0], tile_edges, 0)
    plan = jnp.concatenate([tile_dst, tile_near, tile_far, tile_live, tile_count])
    smem = pl.BlockSpec(memory_space=pltpu.SMEM)
    vmem = pl.BlockSpec(memory_space=pltpu.VMEM)
    return pl.pallas_call(
        mean_kernel,
        out_shape=jax.ShapeDtypeStruct((parts, rows, nodes // parts), features.dtype),
        in_specs=[smem] + [vmem] * 6,
        out_specs=vmem,
        scratch_shapes=[
            pltpu.VMEM((own + 2 * halo_low.shape[0], rows, BLOCK), features.dtype),
            pltpu.VMEM((own, rows + 8, BLOCK), jnp.float32),
        ],
        compiler_params=pltpu.CompilerParams(vmem_limit_bytes=32 * 1024 * 1024),
        name="neighbour_mean",
    )(plan, features, edge_src, edge_dst, hub_rows, halo_low, halo_high)


def project(shares, weights, bias):
    parts, rows, width = shares.shape
    total = jnp.dot(weights, shares.reshape(parts * rows, width), preferred_element_type=jnp.float32)
    updated = jnp.maximum(total + bias[:, None], 0.0).astype(shares.dtype)
    return updated.reshape(parts, rows // 2, width)


def shards(
    features,
    w_self,
    w_neigh,
    bias,
    hub_pick,
    halo_send,
    tile_dst,
    tile_src,
    tile_edges,
    tile_count,
    edge_src,
    edge_dst,
):
    rows, nodes = features.shape
    parts = lax.axis_size("feat")
    count = lax.axis_size("graph")
    hub_local, to_previous, to_next = pick_blocks(features, hub_pick, halo_send)

    along_z = [[X * z + x for z in range(r, Z, STRIDE)] for r in range(STRIDE) for x in range(X)]
    nearby = [
        [X * (z + r) + x for r in range(STRIDE) for x in range(X)] for z in range(0, Z, STRIDE)
    ]
    column = lax.all_gather(hub_local, "graph", axis_index_groups=along_z)
    column, features, tile_src, tile_edges, w_self, w_neigh = lax.optimization_barrier(
        (column, features, tile_src, tile_edges, w_self, w_neigh)
    )
    weights = jnp.stack(
        [w_self.reshape(-1, parts, rows), w_neigh.reshape(-1, parts, rows)], axis=2
    ).reshape(-1, 2 * parts * rows)
    spread = jnp.broadcast_to(column[None], (X * STRIDE, *column.shape))
    hub_rows = lax.all_to_all(spread, "graph", 0, 0, axis_index_groups=nearby)
    hub_rows = hub_rows.reshape(-1, rows, BLOCK)

    forward = [(i, (i + 1) % count) for i in range(count)]
    backward = [(target, source) for source, target in forward]
    halo_low = lax.ppermute(to_next, "graph", forward)
    halo_high = lax.ppermute(to_previous, "graph", backward)

    split = jnp.transpose(features.reshape(rows, parts, nodes // parts), (1, 0, 2))
    hub_rows, weights, split = lax.optimization_barrier((hub_rows, weights, split))
    shares = neighbour_mean(
        features, hub_rows, halo_low, halo_high, tile_dst, tile_src, tile_edges, tile_count, edge_src, edge_dst, parts
    )
    shares = lax.all_to_all(jnp.concatenate([split, shares], axis=1), "feat", 0, 0)
    updated = lax.all_to_all(project(shares, weights, bias), "feat", 0, 0)
    return jnp.transpose(updated, (1, 0, 2)).reshape(rows, nodes)


def solution(mesh):
    in_specs = (
        P("feat", "graph"),
        P(),
        P(),
        P(),
        P("graph"),
        P("graph"),
        P("graph"),
        P("graph"),
        P("graph"),
        P("graph"),
        P("graph", None),
        P("graph", None),
    )
    out_specs = P("feat", "graph")
    return jax.shard_map(shards, mesh=mesh, in_specs=in_specs, out_specs=out_specs, check_vma=False)
```
